32 devices in a mesh: rep: 8 (over z, x), fsdp: 4 (over y, core).
Axes of the slice: x: 2, y: 2, z: 4, core: 2. Of those that a mesh axis runs over, the one named last changes fastest.
Arguments:
- tokens: bfloat16 [4096, 768], P(('rep', 'fsdp')), may hold values from -6 to 6
- expert_ids: int32 [4096, 1], P(('rep', 'fsdp')), may hold values from 0 to 1; in each aligned block of 128 rows (0 to 127, 128 to 255, ...) at most 68 rows name the same one
- seq_lengths: int32 [8, 2], P('rep'), may hold values from 1 to 432, 496 in all within a row
- rel_buckets: int32 [1023], replicated, may hold values from 0 to 31, as said below
- attn_qkv: bfloat16 [3, 768, 768], P(None, 'fsdp'), may hold values from -0.21875 to 0.21875
- attn_out: bfloat16 [768, 768], P('fsdp'), may hold values from -4 to 4
- norm_gains: bfloat16 [2, 768], P(None, 'fsdp'), may hold values from 0.099609375 to 1.8984375
- bias_table: bfloat16 [32, 12], P('fsdp'), may hold values from -4 to 4
- router: bfloat16 [768, 2], P('fsdp'), may hold values from -0.21875 to 0.21875
- w_in: bfloat16 [2, 768, 3072], P(None, None, 'fsdp'), may hold values from -0.21875 to 0.21875
- w_out: bfloat16 [2, 3072, 768], P(None, 'fsdp'), may hold values from -0.21875 to 0.21875
- cotangent: bfloat16 [4096, 768], P(('rep', 'fsdp')), may hold values from -6 to 6
Outputs:
- mixed: bfloat16 [4096, 768], P(('rep', 'fsdp'))
- grad_tokens: float32 [4096, 768], P(('rep', 'fsdp'))
- grad_qkv: float32 [3, 768, 768], P(None, ('rep', 'fsdp'))
- grad_out: float32 [768, 768], P(('rep', 'fsdp'))
- grad_gains: float32 [2, 768], P(None, 'fsdp')
- grad_table: float32 [32, 12], P('fsdp')
- grad_router: float32 [768, 2], P('fsdp')
- grad_w_in: float32 [2, 768, 3072], P(None, 'rep', 'fsdp')
- grad_w_out: float32 [2, 3072, 768], P(None, ('rep', 'fsdp'))
The draws below stay inside these ranges and needn't reach their ends.
Inputs may be any that keep to these rules, and one draw needn't show every extreme that they name: `expert_ids`: each row names the expert of its token; the 128 rows of one device name one expert at most 68 times. `seq_lengths`: row g lists in order the lengths of the sequences packed into the 512 places of group g; they sum to 496, the remaining places are padding that attends only to padding, and none is longer than 432. `rel_buckets`: entry 511 + r is the bucket of the relative position r = key place minus query place.
All inputs are finite; a program needn't handle non-finite values.
Results may differ from the reference program's by a relative error of at most 0.015.
Values may be sent and summed in bfloat16 or wider, within the bound.
A program may use at most 192 MiB of HBM per device.

```python
import math
import jax
import jax.numpy as jnp
import numpy as np
from jax import lax

D = 768
H = 12
HD = 64
FF = 3072
NB = 32
EXPERTS = 2
NSEQ = 2
TOK_DEV = 128
CAP = 68
GRP = 512
PAD = 16
SPAN = 432
TOKENS = 4096
N_REP = 8


def draw_rel_buckets(key, part):
    key = jax.random.fold_in(key, 7)
    half_count = NB // 2
    marks = jnp.sort(jax.random.permutation(key, 119)[:half_count - 9] + 9).astype(jnp.int32)
    offsets = jnp.arange(2 * GRP - 1, dtype=jnp.int32) - (GRP - 1)
    distance = jnp.abs(offsets)
    beyond = 8 + jnp.sum((distance[:, None] >= marks[None, :]).astype(jnp.int32), axis=1)
    level = jnp.where(distance < 8, distance, beyond)
    return (level + half_count * (offsets > 0).astype(jnp.int32)).astype(jnp.int32)


def levels(key, shape, cuts, smallest, high):
    def one(axis_at, blocks):
        heights = jax.random.uniform(jax.random.fold_in(jax.random.fold_in(key, 6), axis_at), (blocks,), jnp.float32, smallest / len(cuts), high / len(cuts))
        return jnp.repeat(jnp.exp(heights), shape[axis_at] // blocks).reshape((-1,) + (1,) * (len(shape) - axis_at - 1))

    loudness = one(*cuts[0])
    for cut in cuts[1:]:
        loudness = loudness * one(*cut)
    return loudness


def length_profile(amount, total, limit, skew):
    portions = [(1 << 20) // math.isqrt(standing ** skew) + 1 for standing in range(2, amount + 1)]
    rest, holding = total - limit - (amount - 1), [1] * (amount - 1)
    while rest > 0:
        free = [i for i in range(amount - 1) if holding[i] < limit]
        pool, remaining = sum([portions[i] for i in free]), rest
        for i in free:
            addition = min(limit - holding[i], max(1, remaining * portions[i] // pool), rest)
            holding[i] = holding[i] + addition
            rest = rest - addition
    return np.array([limit] + holding)


def ragged(key, count, total, reach, lean):
    if count == 2:
        one = jax.random.randint(key, (), max(1, total - reach), min(reach, total - 1) + 1)
        return jnp.stack([one, total - one])
    sizes = jnp.asarray(length_profile(count, total, reach, lean), jnp.int32)
    twos = (count - 1) // 2
    giver, receiver = sizes[1:1 + 2 * twos:2], sizes[2:2 + 2 * twos:2]
    room = jnp.minimum(giver - 1, reach - receiver)
    shifted = jax.random.randint(jax.random.fold_in(key, 1), (twos,), 0, 1 << 20) % (room + 1)
    sizes = sizes.at[1:1 + 2 * twos:2].set(giver - shifted).at[2:2 + 2 * twos:2].set(receiver + shifted)
    return sizes[jax.random.permutation(jax.random.fold_in(key, 2), count)]


def deal_out(rng, own, number, rows, amount, top, bound, slope):
    sequence = jax.random.permutation(rng, amount)
    heavy_load, usual = load_shares(amount, rows * top, bound, slope, True), load_shares(amount, rows * top, bound, slope, False)
    places = jnp.arange(amount)

    def named(sizes, offset_by):
        used = int((sizes > 0).sum())
        fixed = max(1, used // 4)
        shifted = fixed + (places - fixed + offset_by * (used - fixed)) % max(1, amount - fixed)
        return jnp.zeros((amount,), jnp.int32).at[sequence[jnp.where(places < fixed, places, shifted)]].set(jnp.asarray(sizes, jnp.int32))

    sizes = jnp.where(number % 4 == 0, named(heavy_load, number // 4), named(usual, number - number // 4 - 1))
    mixed = jax.random.permutation(jax.random.fold_in(own, 3), amount)
    source_of, sink = mixed[0:amount // 2 * 2:2], mixed[1:amount // 2 * 2:2]
    slack = jnp.minimum(sizes[source_of] - 1, bound - sizes[sink]) // 2
    slack = jnp.where((source_of == sequence[0]) | (sink == sequence[0]) | (sizes[sink] == 0), 0, jnp.maximum(slack, 0))
    shifted = jax.random.randint(jax.random.fold_in(own, 4), (amount // 2,), 0, 1 << 20) % (slack + 1)
    sizes = sizes.at[source_of].add(-shifted).at[sink].add(shifted)
    labels = jnp.searchsorted(jnp.cumsum(sizes), jnp.arange(rows * top), side="right").astype(jnp.int32)
    grid = labels.reshape(top, rows).T
    grid = grid[jax.random.permutation(jax.random.fold_in(own, 1), rows)]
    offset_by = jax.random.randint(jax.random.fold_in(own, 2), (rows, 1), 0, top)
    return jnp.take_along_axis(grid, (jnp.arange(top)[None, :] + offset_by) % top, axis=1)


def load_shares(number_of, total, limit, lean, full):
    loads = [(1 << 20) // math.isqrt(standing ** lean) + 1 for standing in range(1, number_of + 1)]
    largest = limit if full else min(limit, max(-(-total // number_of), total * loads[0] // sum(loads)))
    least = 1 if total - largest >= number_of - 1 else 0
    holding, spare = [largest] + [least] * (number_of - 1), total - largest - least * (number_of - 1)
    while spare > 0:
        free = [i for i in range(1, number_of) if holding[i] < largest] or [i for i in range(1, number_of) if holding[i] < limit]
        pool, remaining = sum([loads[i] for i in free]), spare
        for i in free:
            extra = min(limit - holding[i], max(1, remaining * loads[i] // pool), spare)
            holding[i] = holding[i] + extra
            spare = spare - extra
    return np.array(holding)


def centred(rng, shape, deviation, reach, cuts=(), held_as=jnp.bfloat16):
    drawn = deviation * jax.random.normal(rng, shape, jnp.float32)
    if cuts:
        drawn = drawn * levels(rng, shape, cuts, -0.22, 0.18)
    return jnp.clip(drawn, -reach, reach).astype(held_as)


def setup_inputs(seed: int = 0) -> dict:
    splits = jax.random.split(jax.random.key(seed), 13)
    tokens = centred(splits[0], (TOKENS, D), 1.0, 6.0, ((0, 32),))
    expert_ids_keys = jax.random.split(jax.random.fold_in(splits[1], 1), TOKENS // TOK_DEV)
    expert_ids_turns = jax.random.permutation(jax.random.fold_in(splits[1], 3), TOKENS // TOK_DEV)
    expert_ids = jax.vmap(lambda own, number: deal_out(jax.random.fold_in(splits[1], 2), own, number, TOK_DEV, EXPERTS, 1, CAP, 1))(expert_ids_keys, expert_ids_turns).reshape((TOKENS, 1))
    seq_lengths = jax.vmap(lambda own: ragged(own, NSEQ, GRP - PAD, SPAN, 2))(jax.random.split(splits[2], N_REP)).reshape((N_REP, NSEQ)).astype(jnp.int32)
    rel_buckets = draw_rel_buckets(jax.random.fold_in(splits[12], 71), 0)
    attn_qkv = centred(splits[4], (3, D, D), D ** -0.5, 0.21875, ((1, 4),))
    attn_out = centred(splits[5], (D, D), (max(1, D // 384)) ** -0.5, 4.0, ((0, 4),))
    norm_gains = jnp.clip(1.0 + 0.18 * jax.random.normal(splits[6], (2, D), jnp.float32), 0.099609375, 1.8984375).astype(jnp.bfloat16)
    bias_table = centred(splits[7], (NB, H), 1.0, 4.0, ((0, 4),))
    router = centred(splits[8], (D, EXPERTS), D ** -0.5, 0.21875, ((0, 4),))
    w_in = centred(splits[9], (EXPERTS, D, FF), D ** -0.5, 0.21875, ((2, 4),))
    w_out = centred(splits[10], (EXPERTS, FF, D), (FF // 4) ** -0.5, 0.21875, ((1, 4),))
    cotangent = centred(splits[11], (TOKENS, D), 1.0, 6.0, ((0, 32),))
    return {"tokens": tokens, "expert_ids": expert_ids, "seq_lengths": seq_lengths, "rel_buckets": rel_buckets, "attn_qkv": attn_qkv, "attn_out": attn_out, "norm_gains": norm_gains, "bias_table": bias_table, "router": router, "w_in": w_in, "w_out": w_out, "cotangent": cotangent}


NORM_EPSILON = 1e-06
SCORE_SCALE = 0.125
MASKED_SCORE = -1000000000.0
HIGHEST_PRECISION = lax.Precision.HIGHEST

@jax.custom_vjp
def low(v):
    return lax.optimization_barrier(v.astype(jnp.bfloat16)).astype(jnp.float32)

@jax.custom_vjp
def low_back(v):
    return v

def low_keep(v):
    return (low(v), None)

def low_pass(kept, grad):
    return (grad,)

def back_keep(v):
    return (v, None)

def back_low(kept, grad):
    return (low(grad),)
low.defvjp(low_keep, low_pass)
low_back.defvjp(back_keep, back_low)

def product(left, right):
    return jnp.dot(left, right, precision=HIGHEST_PRECISION, preferred_element_type=jnp.float32)

def norm_rows(values, weights):
    return values * lax.rsqrt(lax.optimization_barrier(jnp.mean(values * values, axis=-1, keepdims=True)) + NORM_EPSILON) * weights

def group_forward(weights, inputs, routes, lengths, rel_buckets):
    qkv, out_proj, gains, table, router, w_in, w_out = weights
    places = jnp.arange(GRP, dtype=jnp.int32)
    seq_ends = jnp.cumsum(lengths)
    seq_ids = lax.optimization_barrier(jnp.sum((places[:, None] >= seq_ends[None, :]).astype(jnp.int32), axis=1))
    normed = low(norm_rows(inputs, gains[0]))
    queries = low(low_back(product(normed, qkv[0]))).reshape(GRP, H, HD)
    keys = low(low_back(product(normed, qkv[1]))).reshape(GRP, H, HD)
    values = low(low_back(product(normed, qkv[2]))).reshape(GRP, H, HD)
    relative = rel_buckets[(places[None, :] - places[:, None] + GRP - 1).astype(jnp.int32)]
    bias = jnp.transpose(table[relative], (2, 0, 1))
    scores = jnp.einsum('qhd,khd->hqk', queries, keys, precision=HIGHEST_PRECISION) * SCORE_SCALE + bias
    scores = low_back(scores)
    scores = jnp.where((seq_ids[:, None] == seq_ids[None, :])[None], scores, MASKED_SCORE)
    probs = jax.nn.softmax(scores, axis=-1)
    attended = jnp.einsum('hqk,khd->qhd', low(probs), values, precision=HIGHEST_PRECISION).reshape(GRP, D)
    attended = low(low_back(attended))
    hidden = inputs + low_back(product(attended, out_proj))
    hidden_normed = low(norm_rows(hidden, gains[1]))
    chosen = (routes == jnp.arange(EXPERTS, dtype=jnp.int32)[None, :]).astype(jnp.float32)
    gating = lax.optimization_barrier(jnp.sum(jax.nn.softmax(product(hidden_normed, router), axis=-1) * chosen, axis=1, keepdims=True))
    routed = jnp.zeros((GRP, D), jnp.float32)
    for index in range(EXPERTS):
        expert_in = low_back(product(hidden_normed, w_in[index]))
        activation = low(jax.nn.gelu(expert_in, approximate=True))
        routed = routed + chosen[:, index:index + 1] * product(activation, w_out[index])
    return hidden + gating * low_back(routed)

def reference(tokens, expert_ids, seq_lengths, rel_buckets, attn_qkv, attn_out, norm_gains, bias_table, router, w_in, w_out, cotangent):
    weights = (attn_qkv.astype(jnp.float32), attn_out.astype(jnp.float32), norm_gains.astype(jnp.float32), bias_table.astype(jnp.float32), router.astype(jnp.float32), w_in.astype(jnp.float32), w_out.astype(jnp.float32))
    route_groups = expert_ids.reshape(N_REP, GRP, 1)

    def forward(inputs, params):

        def one_group(pieces):
            return group_forward(params, pieces[0], pieces[1], pieces[2], rel_buckets)
        result = lax.map(jax.checkpoint(one_group), (inputs.reshape(N_REP, GRP, D), route_groups, seq_lengths))
        return result.reshape(TOKENS, D)
    mixed, pull = jax.vjp(forward, tokens.astype(jnp.float32), weights)
    grad_tokens, grads = pull(cotangent.astype(jnp.float32))
    return (mixed.astype(jnp.bfloat16), grad_tokens, grads[0], grads[1], grads[2], grads[3], grads[4], grads[5], grads[6])
```

```python
from functools import partial

import jax
import jax.numpy as jnp
from jax import lax
from jax.experimental import pallas as pl
from jax.experimental.pallas import tpu as pltpu
from jax.sharding import PartitionSpec as P

D = 768
H = 12
HD = 64
FF = 3072
NB = 32
EXPERTS = 2

NORM_EPSILON = 1e-06
SCORE_SCALE = 0.125
MASKED_SCORE = -1000000000.0
HIGHEST_PRECISION = lax.Precision.HIGHEST
BF = jnp.bfloat16
F32 = jnp.float32


def norm_rows(values, weights):
    return (
        values
        * lax.rsqrt(jnp.mean(values * values, axis=-1, keepdims=True) + NORM_EPSILON)
        * weights
    )


def product(left, right):
    return jnp.dot(left, right, preferred_element_type=F32)


def product_tn(left, right):
    return lax.dot_general(left, right, (((0,), (0,)), ((), ())), preferred_element_type=F32)


def product_nt(left, right):
    return lax.dot_general(left, right, (((1,), (1,)), ((), ())), preferred_element_type=F32)


def forward_kernel(
    lengths, x_ref, gain_ref, w_ref, along_ref, xn_ref, q_ref, k_ref, v_ref, p_ref, a_ref
):
    rows = x_ref.shape[0]
    span = along_ref.shape[1]
    normed = norm_rows(x_ref[...].astype(F32), gain_ref[...].astype(F32)).astype(BF)
    xn_ref[...] = normed
    q_ref[...] = product(normed, w_ref[0]).astype(BF)
    k_ref[...] = product(normed, w_ref[1]).astype(BF)
    v_ref[...] = product(normed, w_ref[2]).astype(BF)
    end_one = lengths[0, 0]
    end_two = end_one + lengths[0, 1]

    def segment(place):
        return (place >= end_one).astype(jnp.int32) + (place >= end_two).astype(jnp.int32)

    seg_rows = segment(lax.broadcasted_iota(jnp.int32, (rows, 1), 0))
    seg_cols = segment(lax.broadcasted_iota(jnp.int32, (1, rows), 1))
    same = seg_rows == seg_cols
    low_row = lax.broadcasted_iota(jnp.int32, (8, span), 0)
    for head in range(p_ref.shape[0]):
        cols = slice(head * HD, (head + 1) * HD)
        start = jnp.broadcast_to(along_ref[head : head + 1, :], (8, span))
        grown = pltpu.roll(start, span - (rows - 1), 1)
        for step in (1, 2, 4):
            grown = jnp.where((low_row & step) != 0, pltpu.roll(grown, step, 1), grown)
        step = 8
        while step < rows:
            grown = jnp.concatenate([grown, pltpu.roll(grown, step, 1)], axis=0)
            step *= 2
        scores = (
            product_nt(q_ref[:, cols], k_ref[:, cols]) * SCORE_SCALE + grown[:, :rows]
        )
        scores = jnp.where(same, scores, MASKED_SCORE)
        raised = jnp.exp(scores - jnp.max(scores, axis=-1, keepdims=True))
        probs = raised / jnp.sum(raised, axis=-1, keepdims=True)
        p_ref[head] = probs
        a_ref[:, cols] = product(probs.astype(BF), v_ref[:, cols]).astype(BF)


def backward_kernel(q_ref, k_ref, v_ref, p_ref, da_ref, dq_ref, dk_ref, dv_ref, along_ref):
    rows = q_ref.shape[0]
    span = along_ref.shape[1]
    low_row = lax.broadcasted_iota(jnp.int32, (8, span), 0)
    along_ref[...] = jnp.zeros_like(along_ref)
    for head in range(p_ref.shape[0]):
        cols = slice(head * HD, (head + 1) * HD)
        probs = p_ref[head]
        grad_att = da_ref[:, cols]
        grad_probs = product_nt(grad_att, v_ref[:, cols])
        total = jnp.sum(probs * grad_probs, axis=-1, keepdims=True)
        grad_scores = (probs * (grad_probs - total)).astype(BF)
        dq_ref[:, cols] = (product(grad_scores, k_ref[:, cols]) * SCORE_SCALE).astype(BF)
        dk_ref[:, cols] = (product_tn(grad_scores, q_ref[:, cols]) * SCORE_SCALE).astype(BF)
        dv_ref[:, cols] = product_tn(probs.astype(BF), grad_att).astype(BF)
        folded = jnp.concatenate(
            [grad_scores.astype(F32), jnp.zeros((rows, span - rows), F32)], axis=1
        )
        half = rows // 2
        while half >= 8:
            folded = folded[:half] + pltpu.roll(folded[half:], span - half, 1)
            half //= 2
        for step in (1, 2, 4):
            folded = jnp.where((low_row & step) != 0, pltpu.roll(folded, span - step, 1), folded)
        summed = pltpu.roll(folded, rows - 1, 1)
        along_ref[head : head + 1, :] = jnp.sum(summed, axis=0, keepdims=True)


def rep_reduce(blocks, order):
    count = blocks.shape[0]
    bits = count.bit_length() - 1
    me = lax.axis_index("rep")
    rest = blocks.shape[1:]
    value = blocks.reshape((2,) * bits + rest)
    left = list(range(bits - 1, -1, -1))
    for bit in order:
        axis = left.index(bit)
        mine = (me >> bit) & 1
        send = lax.dynamic_index_in_dim(value, 1 - mine, axis, keepdims=False).astype(BF)
        keep = lax.dynamic_index_in_dim(value, mine, axis, keepdims=False).astype(F32)
        taken = lax.ppermute(send, "rep", [(i, i ^ (1 << bit)) for i in range(count)])
        value = keep + taken.astype(F32)
        left.remove(bit)
    return value


def to_owner(value):
    rep_count = lax.axis_size("rep")
    fsdp_count = lax.axis_size("fsdp")
    pairs = [
        (r * fsdp_count + f, f * rep_count + r)
        for r in range(rep_count)
        for f in range(fsdp_count)
    ]
    return lax.ppermute(value.astype(BF), ("rep", "fsdp"), pairs).astype(F32)


def local(
    tokens,
    expert_ids,
    seq_lengths,
    rel_buckets,
    attn_qkv,
    attn_out,
    norm_gains,
    bias_table,
    router,
    w_in,
    w_out,
    cotangent,
):
    rows = tokens.shape[0]
    fc = lax.axis_size("fsdp")
    rc = lax.axis_size("rep")
    f = lax.axis_index("fsdp")
    group = rows * fc
    width = D // fc
    heads = H // fc
    span = 2 * group

    vm = pl.BlockSpec(memory_space=pltpu.VMEM)
    bits = rc.bit_length() - 1
    x_first = list(range(bits))
    z_first = ([1, 0] + list(range(2, bits))) if bits > 1 else x_first

    def own(values):
        return lax.dynamic_slice_in_dim(values, f * rows, rows, 0)

    n_gain, n_table, n_router = 2 * width, NB // fc * H, width * EXPERTS
    small = jnp.concatenate(
        [
            norm_gains.reshape(-1),
            bias_table.reshape(-1),
            router.reshape(-1),
            expert_ids[:, 0].astype(BF),
        ]
    )
    small = jnp.pad(small, (0, 2 * D - small.shape[0]))[None]
    pack = jnp.concatenate(
        [
            jnp.concatenate([tokens, cotangent], axis=1),
            jnp.pad(small, ((0, 15), (0, 0))),
        ],
        axis=0,
    )
    got = lax.all_gather(pack, "fsdp")
    x_all = got[:, :rows, :D].reshape(group, D)
    g_all = got[:, :rows, D:].reshape(group, D).astype(F32)
    sm = got[:, rows]
    gains = sm[:, :n_gain].reshape(fc, 2, width).transpose(1, 0, 2).reshape(2, D)
    at = n_gain
    table = sm[:, at : at + n_table].reshape(NB, H)
    at += n_table
    router_full = sm[:, at : at + n_router].reshape(D, EXPERTS)
    at += n_router
    ids_all = sm[:, at : at + rows].reshape(group, 1).astype(F32)

    cut = attn_qkv.reshape(3, width, fc, width).transpose(2, 0, 1, 3)
    qkv_cols = lax.all_to_all(cut, "fsdp", 0, 0, tiled=True)
    qkv_cols = qkv_cols.transpose(1, 0, 2, 3).reshape(3, D, width)
    out_full = lax.all_gather(attn_out, "fsdp", axis=0, tiled=True)

    codes = (
        jnp.pad(rel_buckets, (0, 1))[:, None] == jnp.arange(NB, dtype=jnp.int32)[None, :]
    )
    table_own = lax.dynamic_slice_in_dim(table, f * heads, heads, 1)
    along = lax.dot_general(
        table_own, codes.astype(BF), (((0,), (1,)), ((), ())), preferred_element_type=F32
    )
    along = jnp.pad(along, ((0, 8 - heads), (0, 0)))

    head_type = jax.ShapeDtypeStruct((group, width), BF)
    normed, queries, keys, values, probs, attended = pl.pallas_call(
        forward_kernel,
        in_specs=[pl.BlockSpec(memory_space=pltpu.SMEM), vm, vm, vm, vm],
        out_specs=[vm] * 6,
        out_shape=[
            jax.ShapeDtypeStruct((group, D), BF),
            head_type,
            head_type,
            head_type,
            jax.ShapeDtypeStruct((heads, group, group), F32),
            head_type,
        ],
        compiler_params=pltpu.CompilerParams(vmem_limit_bytes=40 << 20),
        name="attention_forward",
    )(seq_lengths, x_all, gains[:1], qkv_cols, along)

    attended_all = lax.all_gather(attended, "fsdp").transpose(1, 0, 2).reshape(group, D)
    inputs = x_all.astype(F32)
    hidden = inputs + product(attended_all, out_full)
    gain_two = gains[1].astype(F32)
    hn = norm_rows(hidden, gain_two).astype(BF)
    logits = product(hn, router_full)

    def gate_of(values, marks):
        return jnp.sum(jax.nn.softmax(values, axis=-1) * marks, axis=1, keepdims=True)

    chosen = (ids_all == jnp.arange(EXPERTS, dtype=F32)[None, :]).astype(F32)
    gating = gate_of(logits, chosen)
    grad_routed = (gating * g_all).astype(BF)
    first = ids_all == 0.0
    gelu = partial(jax.nn.gelu, approximate=True)
    u = jnp.where(first, product(hn, w_in[0]), product(hn, w_in[1]))
    act, gelu_pull = jax.vjp(gelu, u)
    act = act.astype(BF)
    none = jnp.zeros((), BF)
    act_zero = jnp.where(first, act, none)
    act_one = jnp.where(first, none, act)
    routed_part = product(act_zero, w_out[0]) + product(act_one, w_out[1])
    grad_act = jnp.where(
        first, product_nt(grad_routed, w_out[0]), product_nt(grad_routed, w_out[1])
    )
    grad_u = gelu_pull(grad_act)[0].astype(BF)
    u_zero = jnp.where(first, grad_u, none)
    u_one = jnp.where(first, none, grad_u)
    hn_part = product_nt(u_zero, w_in[0]) + product_nt(u_one, w_in[1])
    parts = jnp.concatenate([routed_part.astype(BF), hn_part.astype(BF)], axis=1)
    parts = lax.all_to_all(parts.reshape(fc, rows, 2 * D), "fsdp", 0, 0, tiled=True)
    sums = jnp.sum(parts.astype(F32), axis=0)
    routed, grad_hn = sums[:, :D], sums[:, D:]

    def blocks_of(pieces, count):
        return jnp.stack(
            [piece.astype(BF).reshape(rc, piece.shape[0] // rc, piece.shape[1]) for piece in pieces],
            axis=1,
        )

    in_share = rep_reduce(
        blocks_of([product_tn(hn, u_zero), product_tn(hn, u_one)], rc), x_first
    )
    outer_share = rep_reduce(
        blocks_of([product_tn(act_zero, grad_routed), product_tn(act_one, grad_routed)], rc),
        z_first,
    )
    grad_w_out = to_owner(outer_share)

    hidden_own = own(hidden)
    hn_own = own(hn)
    logits_own = own(logits)
    chosen_own = own(chosen)
    gating_own = own(gating)
    grad_mixed = cotangent.astype(F32)
    mixed = (hidden_own + gating_own * routed).astype(BF)
    grad_gate = jnp.sum(grad_mixed * routed, axis=1, keepdims=True)
    grad_logits = jax.vjp(lambda z: gate_of(z, chosen_own), logits_own)[1](grad_gate)[0]
    router_wide = router_full.astype(F32)
    grad_hn = grad_hn + (
        grad_logits[:, :1] * router_wide[:, 0][None] + grad_logits[:, 1:] * router_wide[:, 1][None]
    )
    grad_router = lax.dot_general(
        hn_own.astype(F32),
        grad_logits,
        (((0,), (0,)), ((), ())),
        precision=HIGHEST_PRECISION,
        preferred_element_type=F32,
    )
    grad_hidden_part, grad_gain_two = jax.vjp(norm_rows, hidden_own, gain_two)[1](grad_hn)
    grad_hidden = grad_mixed + grad_hidden_part
    branch_all = lax.all_gather(grad_hidden.astype(BF), "fsdp", axis=0, tiled=True)
    grad_attended = product_nt(branch_all, attn_out).astype(BF)
    out_part = product_tn(attended, branch_all).astype(BF)
    out_share = to_owner(rep_reduce(out_part.reshape(rc, width // rc, D), x_first))

    grad_q, grad_k, grad_v, grad_along = pl.pallas_call(
        backward_kernel,
        in_specs=[vm] * 5,
        out_specs=[vm] * 4,
        out_shape=[
            head_type,
            head_type,
            head_type,
            jax.ShapeDtypeStruct((8, span), F32),
        ],
        compiler_params=pltpu.CompilerParams(vmem_limit_bytes=40 << 20),
        name="attention_backward",
    )(queries, keys, values, probs, grad_attended)

    xn_part = (
        product_nt(grad_q, qkv_cols[0])
        + product_nt(grad_k, qkv_cols[1])
        + product_nt(grad_v, qkv_cols[2])
    ).astype(BF)
    xn_parts = lax.all_to_all(xn_part.reshape(fc, rows, D), "fsdp", 0, 0, tiled=True)
    grad_normed = jnp.sum(xn_parts.astype(F32), axis=0)

    grad_stack = jnp.concatenate([grad_q, grad_k, grad_v], axis=1)
    qkv_part = product_tn(normed, grad_stack).astype(BF)
    qkv_share = rep_reduce(qkv_part.reshape(rc, D // rc, 3 * width), x_first)
    piece = D // (rc * fc)
    qkv_share = lax.all_to_all(
        qkv_share.astype(BF).reshape(fc, piece, 3 * width), "fsdp", 0, 0, tiled=True
    )
    grad_qkv = (
        qkv_share.astype(F32)
        .reshape(fc, piece, 3, width)
        .transpose(2, 1, 0, 3)
        .reshape(3, piece, D)
    )

    gain_one = gains[0].astype(F32)
    grad_input_part, grad_gain_one = jax.vjp(norm_rows, tokens.astype(F32), gain_one)[1](
        grad_normed
    )
    grad_tokens = grad_hidden + grad_input_part
    table_own_grad = lax.dot_general(
        codes.astype(F32),
        grad_along[:heads],
        (((0,), (1,)), ((), ())),
        precision=HIGHEST_PRECISION,
        preferred_element_type=F32,
    )
    table_grad = lax.dynamic_update_slice_in_dim(
        jnp.zeros((NB, H), F32), table_own_grad, f * heads, 1
    )
    little = jnp.concatenate(
        [
            grad_gain_one,
            grad_gain_two,
            grad_router.T.reshape(-1),
            table_grad.reshape(-1),
        ]
    ).reshape(-1, 128)
    little = lax.psum(little, ("rep", "fsdp")).reshape(-1)
    grad_gains = lax.dynamic_slice_in_dim(little[: 2 * D].reshape(2, D), f * width, width, 1)
    grad_router = lax.dynamic_slice_in_dim(
        little[2 * D : 4 * D].reshape(EXPERTS, D), f * width, width, 1
    ).T
    grad_table = lax.dynamic_slice_in_dim(
        little[4 * D :].reshape(NB, H), f * (NB // fc), NB // fc, 0
    )
    return (
        mixed,
        grad_tokens,
        grad_qkv,
        out_share,
        grad_gains,
        grad_table,
        grad_router,
        in_share,
        grad_w_out,
    )


def solution(mesh):
    return jax.shard_map(
        local,
        mesh=mesh,
        in_specs=(
            P(("rep", "fsdp"), None),
            P(("rep", "fsdp"), None),
            P("rep", None),
            P(),
            P(None, "fsdp", None),
            P("fsdp", None),
            P(None, "fsdp"),
            P("fsdp", None),
            P("fsdp", None),
            P(None, None, "fsdp"),
            P(None, "fsdp", None),
            P(("rep", "fsdp"), None),
        ),
        out_specs=(
            P(("rep", "fsdp"), None),
            P(("rep", "fsdp"), None),
            P(None, ("rep", "fsdp"), None),
            P(("rep", "fsdp"), None),
            P(None, "fsdp"),
            P("fsdp", None),
            P("fsdp", None),
            P(None, "rep", "fsdp"),
            P(None, ("rep", "fsdp"), None),
        ),
        check_vma=False,
    )
```

```python
from functools import partial

import jax
import jax.numpy as jnp
from jax import lax
from jax.experimental import pallas as pl
from jax.experimental.pallas import tpu as pltpu
from jax.sharding import PartitionSpec as P

D = 768
H = 12
HD = 64
FF = 3072
NB = 32
EXPERTS = 2

NORM_EPSILON = 1e-06
SCORE_SCALE = 0.125
MASKED_SCORE = -1000000000.0
HIGHEST_PRECISION = lax.Precision.HIGHEST
BF = jnp.bfloat16
F32 = jnp.float32


def norm_rows(values, weights):
    return (
        values
        * lax.rsqrt(jnp.mean(values * values, axis=-1, keepdims=True) + NORM_EPSILON)
        * weights
    )


def product(left, right):
    return jnp.dot(left, right, preferred_element_type=F32)


def product_tn(left, right):
    return lax.dot_general(left, right, (((0,), (0,)), ((), ())), preferred_element_type=F32)


def product_nt(left, right):
    return lax.dot_general(left, right, (((1,), (1,)), ((), ())), preferred_element_type=F32)


def forward_kernel(
    lengths, x_ref, gain_ref, w_ref, along_ref, xn_ref, q_ref, k_ref, v_ref, p_ref, a_ref
):
    rows = x_ref.shape[0]
    span = along_ref.shape[1]
    normed = norm_rows(x_ref[...].astype(F32), gain_ref[...].astype(F32)).astype(BF)
    xn_ref[...] = normed
    q_ref[...] = product(normed, w_ref[0]).astype(BF)
    k_ref[...] = product(normed, w_ref[1]).astype(BF)
    v_ref[...] = product(normed, w_ref[2]).astype(BF)
    end_one = lengths[0, 0]
    end_two = end_one + lengths[0, 1]

    def segment(place):
        return (place >= end_one).astype(jnp.int32) + (place >= end_two).astype(jnp.int32)

    seg_rows = segment(lax.broadcasted_iota(jnp.int32, (rows, 1), 0))
    seg_cols = segment(lax.broadcasted_iota(jnp.int32, (1, rows), 1))
    same = seg_rows == seg_cols
    low_row = lax.broadcasted_iota(jnp.int32, (8, span), 0)
    for head in range(p_ref.shape[0]):
        cols = slice(head * HD, (head + 1) * HD)
        start = jnp.broadcast_to(along_ref[head : head + 1, :], (8, span))
        grown = pltpu.roll(start, span - (rows - 1), 1)
        for step in (1, 2, 4):
            grown = jnp.where((low_row & step) != 0, pltpu.roll(grown, step, 1), grown)
        step = 8
        while step < rows:
            grown = jnp.concatenate([grown, pltpu.roll(grown, step, 1)], axis=0)
            step *= 2
        scores = (
            product_nt(q_ref[:, cols], k_ref[:, cols]) * SCORE_SCALE + grown[:, :rows]
        )
        scores = jnp.where(same, scores, MASKED_SCORE)
        raised = jnp.exp(scores - jnp.max(scores, axis=-1, keepdims=True))
        probs = raised / jnp.sum(raised, axis=-1, keepdims=True)
        p_ref[head] = probs
        a_ref[:, cols] = product(probs.astype(BF), v_ref[:, cols]).astype(BF)


def backward_kernel(q_ref, k_ref, v_ref, p_ref, da_ref, dq_ref, dk_ref, dv_ref, along_ref):
    rows = q_ref.shape[0]
    span = along_ref.shape[1]
    low_row = lax.broadcasted_iota(jnp.int32, (8, span), 0)
    along_ref[...] = jnp.zeros_like(along_ref)
    for head in range(p_ref.shape[0]):
        cols = slice(head * HD, (head + 1) * HD)
        probs = p_ref[head]
        grad_att = da_ref[:, cols]
        grad_probs = product_nt(grad_att, v_ref[:, cols])
        total = jnp.sum(probs * grad_probs, axis=-1, keepdims=True)
        grad_scores = (probs * (grad_probs - total)).astype(BF)
        dq_ref[:, cols] = (product(grad_scores, k_ref[:, cols]) * SCORE_SCALE).astype(BF)
        dk_ref[:, cols] = (product_tn(grad_scores, q_ref[:, cols]) * SCORE_SCALE).astype(BF)
        dv_ref[:, cols] = product_tn(probs.astype(BF), grad_att).astype(BF)
        folded = jnp.concatenate(
            [grad_scores.astype(F32), jnp.zeros((rows, span - rows), F32)], axis=1
        )
        half = rows // 2
        while half >= 8:
            folded = folded[:half] + pltpu.roll(folded[half:], span - half, 1)
            half //= 2
        for step in (1, 2, 4):
            folded = jnp.where((low_row & step) != 0, pltpu.roll(folded, span - step, 1), folded)
        summed = pltpu.roll(folded, rows - 1, 1)
        along_ref[head : head + 1, :] = jnp.sum(summed, axis=0, keepdims=True)


def rep_blocks(blocks):
    bits = blocks.shape[0].bit_length() - 1
    return blocks.reshape((2,) * bits + blocks.shape[1:]), list(range(bits - 1, -1, -1))


def rep_step(value, left, bit):
    count = lax.axis_size("rep")
    axis = left.index(bit)
    mine = (lax.axis_index("rep") >> bit) & 1
    send = lax.dynamic_index_in_dim(value, 1 - mine, axis, keepdims=False).astype(BF)
    keep = lax.dynamic_index_in_dim(value, mine, axis, keepdims=False).astype(F32)
    taken = lax.ppermute(send, "rep", [(i, i ^ (1 << bit)) for i in range(count)])
    return keep + taken.astype(F32), [other for other in left if other != bit]


def rep_reduce(value, left, order):
    for bit in order:
        value, left = rep_step(value, left, bit)
    return value


def rep_sum(value):
    count = lax.axis_size("rep")
    bit = 1
    while bit < count:
        value = value + lax.ppermute(value, "rep", [(i, i ^ bit) for i in range(count)])
        bit *= 2
    return value


def to_owner(value):
    rep_count = lax.axis_size("rep")
    fsdp_count = lax.axis_size("fsdp")
    pairs = [
        (r * fsdp_count + f, f * rep_count + r)
        for r in range(rep_count)
        for f in range(fsdp_count)
    ]
    return lax.ppermute(value.astype(BF), ("rep", "fsdp"), pairs).astype(F32)


def local(
    tokens,
    expert_ids,
    seq_lengths,
    rel_buckets,
    attn_qkv,
    attn_out,
    norm_gains,
    bias_table,
    router,
    w_in,
    w_out,
    cotangent,
):
    rows = tokens.shape[0]
    fc = lax.axis_size("fsdp")
    rc = lax.axis_size("rep")
    f = lax.axis_index("fsdp")
    group = rows * fc
    width = D // fc
    heads = H // fc
    span = 2 * group

    vm = pl.BlockSpec(memory_space=pltpu.VMEM)
    bits = rc.bit_length() - 1
    x_first = list(range(bits))
    z_first = ([1, 0] + list(range(2, bits))) if bits > 1 else x_first

    def own(values):
        return lax.dynamic_slice_in_dim(values, f * rows, rows, 0)

    n_gain, n_table, n_router = 2 * width, NB // fc * H, width * EXPERTS
    small = jnp.concatenate(
        [
            norm_gains.reshape(-1),
            bias_table.reshape(-1),
            router.reshape(-1),
            expert_ids[:, 0].astype(BF),
        ]
    )
    small = jnp.pad(small, (0, 2 * D - small.shape[0]))
    small = small.reshape(2, D)
    pack = jnp.concatenate([tokens, jnp.pad(small, ((0, 14), (0, 0)))], axis=0)
    got = lax.all_gather(pack, "fsdp", axis=0, tiled=True).reshape(fc, rows + 16, D)
    x_all = got[:, :rows].reshape(group, D)
    g_all = lax.all_gather(cotangent, "fsdp", axis=0, tiled=True).astype(F32)
    sm = got[:, rows : rows + 2].reshape(fc, 2 * D)
    gains = sm[:, :n_gain].reshape(fc, 2, width).transpose(1, 0, 2).reshape(2, D)
    at = n_gain
    table = sm[:, at : at + n_table].reshape(NB, H)
    at += n_table
    router_full = sm[:, at : at + n_router].reshape(D, EXPERTS)
    at += n_router
    ids_all = sm[:, at : at + rows].reshape(group, 1).astype(F32)

    cut = attn_qkv.reshape(3, width, fc, width).transpose(2, 0, 1, 3)
    qkv_cols = lax.all_to_all(cut, "fsdp", 0, 0, tiled=True)
    qkv_cols = qkv_cols.transpose(1, 0, 2, 3).reshape(3, D, width)
    out_full = lax.all_gather(attn_out, "fsdp", axis=0, tiled=True)

    codes = (
        jnp.pad(rel_buckets, (0, 1))[:, None] == jnp.arange(NB, dtype=jnp.int32)[None, :]
    )
    table_own = lax.dynamic_slice_in_dim(table, f * heads, heads, 1)
    along = lax.dot_general(
        table_own, codes.astype(BF), (((0,), (1,)), ((), ())), preferred_element_type=F32
    )
    along = jnp.pad(along, ((0, 8 - heads), (0, 0)))

    head_type = jax.ShapeDtypeStruct((group, width), BF)
    normed, queries, keys, values, probs, attended = pl.pallas_call(
        forward_kernel,
        in_specs=[pl.BlockSpec(memory_space=pltpu.SMEM), vm, vm, vm, vm],
        out_specs=[vm] * 6,
        out_shape=[
            jax.ShapeDtypeStruct((group, D), BF),
            head_type,
            head_type,
            head_type,
            jax.ShapeDtypeStruct((heads, group, group), F32),
            head_type,
        ],
        compiler_params=pltpu.CompilerParams(vmem_limit_bytes=40 << 20),
        name="attention_forward",
    )(seq_lengths, x_all, gains[:1], qkv_cols, along)

    attended_all = lax.all_gather(attended, "fsdp").transpose(1, 0, 2).reshape(group, D)
    inputs = x_all.astype(F32)
    hidden = inputs + product(attended_all, out_full)
    gain_two = gains[1].astype(F32)
    hn = norm_rows(hidden, gain_two).astype(BF)
    logits = product(hn, router_full)

    def gate_of(values, marks):
        return jnp.sum(jax.nn.softmax(values, axis=-1) * marks, axis=1, keepdims=True)

    chosen = (ids_all == jnp.arange(EXPERTS, dtype=F32)[None, :]).astype(F32)
    gating = gate_of(logits, chosen)
    grad_routed = (gating * g_all).astype(BF)
    first = ids_all == 0.0
    gelu = partial(jax.nn.gelu, approximate=True)
    u = jnp.where(first, product(hn, w_in[0]), product(hn, w_in[1]))
    act, gelu_pull = jax.vjp(gelu, u)
    act = act.astype(BF)
    none = jnp.zeros((), BF)
    act_zero = jnp.where(first, act, none)
    act_one = jnp.where(first, none, act)
    routed_part = product(act_zero, w_out[0]) + product(act_one, w_out[1])
    grad_act = jnp.where(
        first, product_nt(grad_routed, w_out[0]), product_nt(grad_routed, w_out[1])
    )
    grad_u = gelu_pull(grad_act)[0].astype(BF)
    u_zero = jnp.where(first, grad_u, none)
    u_one = jnp.where(first, none, grad_u)
    hn_part = product_nt(u_zero, w_in[0]) + product_nt(u_one, w_in[1])
    parts = jnp.concatenate([routed_part.astype(BF), hn_part.astype(BF)], axis=1)
    parts = lax.all_to_all(parts.reshape(fc, rows, 2 * D), "fsdp", 0, 0, tiled=True)
    sums = jnp.sum(parts.astype(F32), axis=0)
    routed, grad_hn = sums[:, :D], sums[:, D:]

    def blocks_of(pieces):
        return jnp.stack(
            [piece.astype(BF).reshape(rc, piece.shape[0] // rc, piece.shape[1]) for piece in pieces],
            axis=1,
        )

    in_value, in_left = rep_step(
        *rep_blocks(blocks_of([product_tn(hn, u_zero), product_tn(hn, u_one)])), x_first[0]
    )
    outer_value, outer_left = rep_step(
        *rep_blocks(
            blocks_of([product_tn(act_zero, grad_routed), product_tn(act_one, grad_routed)])
        ),
        z_first[0],
    )

    hidden_own = own(hidden)
    hn_own = own(hn)
    logits_own = own(logits)
    chosen_own = own(chosen)
    gating_own = own(gating)
    grad_mixed = cotangent.astype(F32)
    mixed = (hidden_own + gating_own * routed).astype(BF)
    grad_gate = jnp.sum(grad_mixed * routed, axis=1, keepdims=True)
    grad_logits = jax.vjp(lambda z: gate_of(z, chosen_own), logits_own)[1](grad_gate)[0]
    router_wide = router_full.astype(F32)
    grad_hn = grad_hn + (
        grad_logits[:, :1] * router_wide[:, 0][None] + grad_logits[:, 1:] * router_wide[:, 1][None]
    )
    grad_router = lax.dot_general(
        hn_own.astype(F32),
        grad_logits,
        (((0,), (0,)), ((), ())),
        precision=HIGHEST_PRECISION,
        preferred_element_type=F32,
    )
    grad_hidden_part, grad_gain_two = jax.vjp(norm_rows, hidden_own, gain_two)[1](grad_hn)
    grad_hidden = grad_mixed + grad_hidden_part
    branch_all = lax.all_gather(grad_hidden.astype(BF), "fsdp", axis=0, tiled=True)
    grad_attended = product_nt(branch_all, attn_out).astype(BF)
    out_part = product_tn(attended, branch_all).astype(BF)
    grad_attended, in_value, outer_value = lax.optimization_barrier(
        (grad_attended, in_value, outer_value)
    )
    in_share = rep_reduce(in_value, in_left, x_first[1:])
    grad_w_out = to_owner(rep_reduce(outer_value, outer_left, z_first[1:]))
    out_share = to_owner(
        rep_reduce(*rep_blocks(out_part.reshape(rc, width // rc, D)), x_first)
    )

    grad_q, grad_k, grad_v, grad_along = pl.pallas_call(
        backward_kernel,
        in_specs=[vm] * 5,
        out_specs=[vm] * 4,
        out_shape=[
            head_type,
            head_type,
            head_type,
            jax.ShapeDtypeStruct((8, span), F32),
        ],
        compiler_params=pltpu.CompilerParams(vmem_limit_bytes=40 << 20),
        name="attention_backward",
    )(queries, keys, values, probs, grad_attended)

    xn_part = (
        product_nt(grad_q, qkv_cols[0])
        + product_nt(grad_k, qkv_cols[1])
        + product_nt(grad_v, qkv_cols[2])
    )
    gain_one = gains[0].astype(F32)
    grad_gain_one = jnp.sum(xn_part * norm_rows(inputs, jnp.ones((), F32)), axis=0)
    table_own_grad = lax.dot_general(
        codes.astype(F32),
        grad_along[:heads],
        (((0,), (1,)), ((), ())),
        precision=HIGHEST_PRECISION,
        preferred_element_type=F32,
    )
    table_grad = lax.dynamic_update_slice_in_dim(
        jnp.zeros((NB, H), F32), table_own_grad, f * heads, 1
    )
    little = jnp.stack([grad_gain_one, grad_gain_two, grad_router[:, 0], grad_router[:, 1]])
    little = jnp.concatenate(
        [
            little.reshape(4, fc, width).transpose(1, 0, 2).reshape(fc, 4 * width),
            table_grad.reshape(fc, NB // fc * H),
        ],
        axis=1,
    )
    n_little = little.shape[1]
    high = little.astype(BF)
    low = (little - high.astype(F32)).astype(BF)
    little = jnp.pad(jnp.concatenate([high, low], axis=1), ((0, 0), (0, 3 * D - 2 * n_little)))
    little = jnp.pad(little.reshape(fc, 3, D), ((0, 0), (0, 13), (0, 0)))
    sent = jnp.concatenate([xn_part.astype(BF).reshape(fc, rows, D), little], axis=1)
    xn_parts = lax.all_to_all(sent, "fsdp", 0, 0, tiled=True)
    grad_normed = jnp.sum(xn_parts[:, :rows].astype(F32), axis=0)
    little = jnp.sum(xn_parts[:, rows : rows + 3].astype(F32), axis=0).reshape(3 * D)
    little = little[:n_little] + little[n_little : 2 * n_little]
    little = rep_sum(jnp.pad(little, (0, 1024 - n_little)).reshape(8, 128)).reshape(-1)
    grad_gains = little[: 2 * width].reshape(2, width)
    grad_router = little[2 * width : 4 * width].reshape(EXPERTS, width).T
    grad_table = little[4 * width : n_little].reshape(NB // fc, H)

    grad_stack = jnp.concatenate([grad_q, grad_k, grad_v], axis=1)
    qkv_part = product_tn(normed, grad_stack).astype(BF)
    qkv_share = rep_reduce(*rep_blocks(qkv_part.reshape(rc, D // rc, 3 * width)), x_first)
    piece = D // (rc * fc)
    qkv_share = lax.all_to_all(
        qkv_share.astype(BF).reshape(fc, piece, 3 * width), "fsdp", 0, 0, tiled=True
    )
    grad_qkv = (
        qkv_share.astype(F32)
        .reshape(fc, piece, 3, width)
        .transpose(2, 1, 0, 3)
        .reshape(3, piece, D)
    )

    grad_input_part = jax.vjp(lambda z: norm_rows(z, gain_one), tokens.astype(F32))[1](
        grad_normed
    )[0]
    grad_tokens = grad_hidden + grad_input_part
    return (
        mixed,
        grad_tokens,
        grad_qkv,
        out_share,
        grad_gains,
        grad_table,
        grad_router,
        in_share,
        grad_w_out,
    )


def solution(mesh):
    return jax.shard_map(
        local,
        mesh=mesh,
        in_specs=(
            P(("rep", "fsdp"), None),
            P(("rep", "fsdp"), None),
            P("rep", None),
            P(),
            P(None, "fsdp", None),
            P("fsdp", None),
            P(None, "fsdp"),
            P("fsdp", None),
            P("fsdp", None),
            P(None, None, "fsdp"),
            P(None, "fsdp", None),
            P(("rep", "fsdp"), None),
        ),
        out_specs=(
            P(("rep", "fsdp"), None),
            P(("rep", "fsdp"), None),
            P(None, ("rep", "fsdp"), None),
            P(("rep", "fsdp"), None),
            P(None, "fsdp"),
            P("fsdp", None),
            P("fsdp", None),
            P(None, "rep", "fsdp"),
            P(None, ("rep", "fsdp"), None),
        ),
        check_vma=False,
    )
```

```python
from functools import partial

import jax
import jax.numpy as jnp
from jax import lax
from jax.experimental import pallas as pl
from jax.experimental.pallas import tpu as pltpu
from jax.sharding import PartitionSpec as P

D = 768
H = 12
HD = 64
FF = 3072
NB = 32
EXPERTS = 2

NORM_EPSILON = 1e-06
SCORE_SCALE = 0.125
MASKED_SCORE = -1000000000.0
HIGHEST_PRECISION = lax.Precision.HIGHEST
BF = jnp.bfloat16
F32 = jnp.float32


def norm_rows(values, weights):
    return (
        values
        * lax.rsqrt(jnp.mean(values * values, axis=-1, keepdims=True) + NORM_EPSILON)
        * weights
    )


def product(left, right):
    return jnp.dot(left, right, preferred_element_type=F32)


def product_tn(left, right):
    return lax.dot_general(left, right, (((0,), (0,)), ((), ())), preferred_element_type=F32)


def product_nt(left, right):
    return lax.dot_general(left, right, (((1,), (1,)), ((), ())), preferred_element_type=F32)


def forward_kernel(
    lengths, x_ref, gain_ref, w_ref, along_ref, xn_ref, q_ref, k_ref, v_ref, p_ref, a_ref
):
    rows = x_ref.shape[0]
    span = along_ref.shape[1]
    normed = norm_rows(x_ref[...].astype(F32), gain_ref[...].astype(F32)).astype(BF)
    xn_ref[...] = normed
    q_ref[...] = product(normed, w_ref[0]).astype(BF)
    k_ref[...] = product(normed, w_ref[1]).astype(BF)
    v_ref[...] = product(normed, w_ref[2]).astype(BF)
    end_one = lengths[0, 0]
    end_two = end_one + lengths[0, 1]

    def segment(place):
        return (place >= end_one).astype(jnp.int32) + (place >= end_two).astype(jnp.int32)

    seg_rows = segment(lax.broadcasted_iota(jnp.int32, (rows, 1), 0))
    seg_cols = segment(lax.broadcasted_iota(jnp.int32, (1, rows), 1))
    same = seg_rows == seg_cols
    low_row = lax.broadcasted_iota(jnp.int32, (8, span), 0)
    for head in range(p_ref.shape[0]):
        cols = slice(head * HD, (head + 1) * HD)
        start = jnp.broadcast_to(along_ref[head : head + 1, :], (8, span))
        grown = pltpu.roll(start, span - (rows - 1), 1)
        for step in (1, 2, 4):
            grown = jnp.where((low_row & step) != 0, pltpu.roll(grown, step, 1), grown)
        step = 8
        while step < rows:
            grown = jnp.concatenate([grown, pltpu.roll(grown, step, 1)], axis=0)
            step *= 2
        scores = (
            product_nt(q_ref[:, cols], k_ref[:, cols]) * SCORE_SCALE + grown[:, :rows]
        )
        scores = jnp.where(same, scores, MASKED_SCORE)
        raised = jnp.exp(scores - jnp.max(scores, axis=-1, keepdims=True))
        probs = raised / jnp.sum(raised, axis=-1, keepdims=True)
        p_ref[head] = probs
        a_ref[:, cols] = product(probs.astype(BF), v_ref[:, cols]).astype(BF)


def backward_kernel(q_ref, k_ref, v_ref, p_ref, da_ref, dq_ref, dk_ref, dv_ref, along_ref):
    rows = q_ref.shape[0]
    span = along_ref.shape[1]
    low_row = lax.broadcasted_iota(jnp.int32, (8, span), 0)
    along_ref[...] = jnp.zeros_like(along_ref)
    for head in range(p_ref.shape[0]):
        cols = slice(head * HD, (head + 1) * HD)
        probs = p_ref[head]
        grad_att = da_ref[:, cols]
        grad_probs = product_nt(grad_att, v_ref[:, cols])
        total = jnp.sum(probs * grad_probs, axis=-1, keepdims=True)
        grad_scores = (probs * (grad_probs - total)).astype(BF)
        dq_ref[:, cols] = (product(grad_scores, k_ref[:, cols]) * SCORE_SCALE).astype(BF)
        dk_ref[:, cols] = (product_tn(grad_scores, q_ref[:, cols]) * SCORE_SCALE).astype(BF)
        dv_ref[:, cols] = product_tn(probs.astype(BF), grad_att).astype(BF)
        folded = jnp.concatenate(
            [grad_scores.astype(F32), jnp.zeros((rows, span - rows), F32)], axis=1
        )
        half = rows // 2
        while half >= 8:
            folded = folded[:half] + pltpu.roll(folded[half:], span - half, 1)
            half //= 2
        for step in (1, 2, 4):
            folded = jnp.where((low_row & step) != 0, pltpu.roll(folded, span - step, 1), folded)
        summed = pltpu.roll(folded, rows - 1, 1)
        along_ref[head : head + 1, :] = jnp.sum(summed, axis=0, keepdims=True)


def rep_blocks(blocks):
    bits = blocks.shape[0].bit_length() - 1
    return blocks.reshape((2,) * bits + blocks.shape[1:]), list(range(bits - 1, -1, -1))


def rep_step(value, left, bit):
    count = lax.axis_size("rep")
    axis = left.index(bit)
    mine = (lax.axis_index("rep") >> bit) & 1
    send = lax.dynamic_index_in_dim(value, 1 - mine, axis, keepdims=False).astype(BF)
    keep = lax.dynamic_index_in_dim(value, mine, axis, keepdims=False).astype(F32)
    taken = lax.ppermute(send, "rep", [(i, i ^ (1 << bit)) for i in range(count)])
    return keep + taken.astype(F32), [other for other in left if other != bit]


def rep_reduce(value, left, order):
    for bit in order:
        value, left = rep_step(value, left, bit)
    return value


def rep_sum(value):
    count = lax.axis_size("rep")
    bit = 1
    while bit < count:
        value = value + lax.ppermute(value, "rep", [(i, i ^ bit) for i in range(count)])
        bit *= 2
    return value


def to_owner(value):
    rep_count = lax.axis_size("rep")
    fsdp_count = lax.axis_size("fsdp")
    pairs = [
        (r * fsdp_count + f, f * rep_count + r)
        for r in range(rep_count)
        for f in range(fsdp_count)
    ]
    return lax.ppermute(value.astype(BF), ("rep", "fsdp"), pairs).astype(F32)


def local(
    tokens,
    expert_ids,
    seq_lengths,
    rel_buckets,
    attn_qkv,
    attn_out,
    norm_gains,
    bias_table,
    router,
    w_in,
    w_out,
    cotangent,
):
    rows = tokens.shape[0]
    fc = lax.axis_size("fsdp")
    rc = lax.axis_size("rep")
    f = lax.axis_index("fsdp")
    group = rows * fc
    width = D // fc
    heads = H // fc
    span = 2 * group

    vm = pl.BlockSpec(memory_space=pltpu.VMEM)
    bits = rc.bit_length() - 1
    x_first = list(range(bits))
    z_first = ([1, 0] + list(range(2, bits))) if bits > 1 else x_first

    def own(values):
        return lax.dynamic_slice_in_dim(values, f * rows, rows, 0)

    n_gain, n_table, n_router = 2 * width, NB // fc * H, width * EXPERTS
    small = jnp.concatenate(
        [
            norm_gains.reshape(-1),
            bias_table.reshape(-1),
            router.reshape(-1),
            expert_ids[:, 0].astype(BF),
        ]
    )
    small = jnp.pad(small, (0, 2 * D - small.shape[0]))
    small = small.reshape(2, D)
    pack = jnp.concatenate([tokens, jnp.pad(small, ((0, 14), (0, 0)))], axis=0)
    got = lax.all_gather(pack, "fsdp", axis=0, tiled=True).reshape(fc, rows + 16, D)
    x_all = got[:, :rows].reshape(group, D)
    later = lax.all_gather(jnp.concatenate([attn_out, cotangent], axis=0), "fsdp")
    out_full = later[:, :width].reshape(D, D)
    g_all = later[:, width:].reshape(group, D).astype(F32)
    sm = got[:, rows : rows + 2].reshape(fc, 2 * D)
    gains = sm[:, :n_gain].reshape(fc, 2, width).transpose(1, 0, 2).reshape(2, D)
    at = n_gain
    table = sm[:, at : at + n_table].reshape(NB, H)
    at += n_table
    router_full = sm[:, at : at + n_router].reshape(D, EXPERTS)
    at += n_router
    ids_all = sm[:, at : at + rows].reshape(group, 1).astype(F32)

    cut = attn_qkv.reshape(3, width, fc, width).transpose(2, 0, 1, 3)
    qkv_cols = lax.all_to_all(cut, "fsdp", 0, 0, tiled=True)
    qkv_cols = qkv_cols.transpose(1, 0, 2, 3).reshape(3, D, width)

    codes = (
        jnp.pad(rel_buckets, (0, 1))[:, None] == jnp.arange(NB, dtype=jnp.int32)[None, :]
    )
    table_own = lax.dynamic_slice_in_dim(table, f * heads, heads, 1)
    along = lax.dot_general(
        table_own, codes.astype(BF), (((0,), (1,)), ((), ())), preferred_element_type=F32
    )
    along = jnp.pad(along, ((0, 8 - heads), (0, 0)))

    head_type = jax.ShapeDtypeStruct((group, width), BF)
    normed, queries, keys, values, probs, attended = pl.pallas_call(
        forward_kernel,
        in_specs=[pl.BlockSpec(memory_space=pltpu.SMEM), vm, vm, vm, vm],
        out_specs=[vm] * 6,
        out_shape=[
            jax.ShapeDtypeStruct((group, D), BF),
            head_type,
            head_type,
            head_type,
            jax.ShapeDtypeStruct((heads, group, group), F32),
            head_type,
        ],
        compiler_params=pltpu.CompilerParams(vmem_limit_bytes=40 << 20),
        name="attention_forward",
    )(seq_lengths, x_all, gains[:1], qkv_cols, along)

    attended_all = lax.all_gather(attended, "fsdp").transpose(1, 0, 2).reshape(group, D)
    inputs = x_all.astype(F32)
    hidden = inputs + product(attended_all, out_full)
    gain_two = gains[1].astype(F32)
    hn = norm_rows(hidden, gain_two).astype(BF)
    logits = product(hn, router_full)

    def gate_of(values, marks):
        return jnp.sum(jax.nn.softmax(values, axis=-1) * marks, axis=1, keepdims=True)

    chosen = (ids_all == jnp.arange(EXPERTS, dtype=F32)[None, :]).astype(F32)
    gating = gate_of(logits, chosen)
    grad_routed = (gating * g_all).astype(BF)
    first = ids_all == 0.0
    gelu = partial(jax.nn.gelu, approximate=True)
    u = jnp.where(first, product(hn, w_in[0]), product(hn, w_in[1]))
    act, gelu_pull = jax.vjp(gelu, u)
    act = act.astype(BF)
    none = jnp.zeros((), BF)
    act_zero = jnp.where(first, act, none)
    act_one = jnp.where(first, none, act)
    routed_part = product(act_zero, w_out[0]) + product(act_one, w_out[1])
    grad_act = jnp.where(
        first, product_nt(grad_routed, w_out[0]), product_nt(grad_routed, w_out[1])
    )
    grad_u = gelu_pull(grad_act)[0].astype(BF)
    u_zero = jnp.where(first, grad_u, none)
    u_one = jnp.where(first, none, grad_u)
    hn_part = product_nt(u_zero, w_in[0]) + product_nt(u_one, w_in[1])
    parts = jnp.concatenate([routed_part.astype(BF), hn_part.astype(BF)], axis=1)
    parts, u_zero, u_one, act_zero, act_one = lax.optimization_barrier(
        (parts, u_zero, u_one, act_zero, act_one)
    )
    parts = lax.all_to_all(parts.reshape(fc, rows, 2 * D), "fsdp", 0, 0, tiled=True)
    sums = jnp.sum(parts.astype(F32), axis=0)
    routed, grad_hn = sums[:, :D], sums[:, D:]

    def blocks_of(pieces):
        return jnp.stack(
            [piece.astype(BF).reshape(rc, piece.shape[0] // rc, piece.shape[1]) for piece in pieces],
            axis=1,
        )

    in_value, in_left = rep_step(
        *rep_blocks(blocks_of([product_tn(hn, u_zero), product_tn(hn, u_one)])), x_first[0]
    )
    outer_value, outer_left = rep_step(
        *rep_blocks(
            blocks_of([product_tn(act_zero, grad_routed), product_tn(act_one, grad_routed)])
        ),
        z_first[0],
    )

    hidden_own = own(hidden)
    hn_own = own(hn)
    logits_own = own(logits)
    chosen_own = own(chosen)
    gating_own = own(gating)
    grad_mixed = cotangent.astype(F32)
    mixed = (hidden_own + gating_own * routed).astype(BF)
    grad_gate = jnp.sum(grad_mixed * routed, axis=1, keepdims=True)
    grad_logits = jax.vjp(lambda z: gate_of(z, chosen_own), logits_own)[1](grad_gate)[0]
    router_wide = router_full.astype(F32)
    grad_hn = grad_hn + (
        grad_logits[:, :1] * router_wide[:, 0][None] + grad_logits[:, 1:] * router_wide[:, 1][None]
    )
    grad_router = lax.dot_general(
        hn_own.astype(F32),
        grad_logits,
        (((0,), (0,)), ((), ())),
        precision=HIGHEST_PRECISION,
        preferred_element_type=F32,
    )
    grad_hidden_part, grad_gain_two = jax.vjp(norm_rows, hidden_own, gain_two)[1](grad_hn)
    grad_hidden = grad_mixed + grad_hidden_part
    branch_all = lax.all_gather(grad_hidden.astype(BF), "fsdp", axis=0, tiled=True)
    grad_attended = product_nt(branch_all, attn_out).astype(BF)
    out_part = product_tn(attended, branch_all).astype(BF)
    grad_attended, in_value, outer_value = lax.optimization_barrier(
        (grad_attended, in_value, outer_value)
    )
    in_value, in_left = rep_step(in_value, in_left, x_first[1])
    outer_value, outer_left = rep_step(outer_value, outer_left, z_first[1])
    out_share = to_owner(
        rep_reduce(*rep_blocks(out_part.reshape(rc, width // rc, D)), x_first)
    )

    grad_q, grad_k, grad_v, grad_along = pl.pallas_call(
        backward_kernel,
        in_specs=[vm] * 5,
        out_specs=[vm] * 4,
        out_shape=[
            head_type,
            head_type,
            head_type,
            jax.ShapeDtypeStruct((8, span), F32),
        ],
        compiler_params=pltpu.CompilerParams(vmem_limit_bytes=40 << 20),
        cost_estimate=pl.CostEstimate(
            flops=10 * heads * group * group * HD,
            bytes_accessed=16 * heads * group * group,
            transcendentals=0,
        ),
        name="attention_backward",
    )(queries, keys, values, probs, grad_attended)

    xn_part = (
        product_nt(grad_q, qkv_cols[0])
        + product_nt(grad_k, qkv_cols[1])
        + product_nt(grad_v, qkv_cols[2])
    )
    gain_one = gains[0].astype(F32)
    grad_gain_one = jnp.sum(xn_part * norm_rows(inputs, jnp.ones((), F32)), axis=0)
    table_own_grad = lax.dot_general(
        codes.astype(F32),
        grad_along[:heads],
        (((0,), (1,)), ((), ())),
        precision=HIGHEST_PRECISION,
        preferred_element_type=F32,
    )
    table_grad = lax.dynamic_update_slice_in_dim(
        jnp.zeros((NB, H), F32), table_own_grad, f * heads, 1
    )
    little = jnp.stack([grad_gain_one, grad_gain_two, grad_router[:, 0], grad_router[:, 1]])
    little = jnp.concatenate(
        [
            little.reshape(4, fc, width).transpose(1, 0, 2).reshape(fc, 4 * width),
            table_grad.reshape(fc, NB // fc * H),
        ],
        axis=1,
    )
    n_little = little.shape[1]
    high = little.astype(BF)
    low = (little - high.astype(F32)).astype(BF)
    little = jnp.pad(jnp.concatenate([high, low], axis=1), ((0, 0), (0, 3 * D - 2 * n_little)))
    little = jnp.pad(little.reshape(fc, 3, D), ((0, 0), (0, 13), (0, 0)))
    sent = jnp.concatenate([xn_part.astype(BF).reshape(fc, rows, D), little], axis=1)
    xn_parts = lax.all_to_all(sent, "fsdp", 0, 0, tiled=True)
    grad_stack = jnp.concatenate([grad_q, grad_k, grad_v], axis=1)
    qkv_part = product_tn(normed, grad_stack).astype(BF)
    qkv_part, in_value, outer_value = lax.optimization_barrier((qkv_part, in_value, outer_value))
    in_share = rep_reduce(in_value, in_left, x_first[2:])
    grad_w_out = to_owner(rep_reduce(outer_value, outer_left, z_first[2:]))
    qkv_value, qkv_left = rep_step(
        *rep_blocks(qkv_part.reshape(rc, D // rc, 3 * width)), x_first[0]
    )
    qkv_value, xn_parts = lax.optimization_barrier((qkv_value, xn_parts))
    qkv_share = rep_reduce(qkv_value, qkv_left, x_first[1:])
    grad_normed = jnp.sum(xn_parts[:, :rows].astype(F32), axis=0)
    little = jnp.sum(xn_parts[:, rows : rows + 3].astype(F32), axis=0).reshape(3 * D)
    little = little[:n_little] + little[n_little : 2 * n_little]
    little = rep_sum(jnp.pad(little, (0, 1024 - n_little)).reshape(8, 128)).reshape(-1)
    grad_gains = little[: 2 * width].reshape(2, width)
    grad_router = little[2 * width : 4 * width].reshape(EXPERTS, width).T
    grad_table = little[4 * width : n_little].reshape(NB // fc, H)

    piece = D // (rc * fc)
    qkv_share = lax.all_to_all(
        qkv_share.astype(BF).reshape(fc, piece, 3 * width), "fsdp", 0, 0, tiled=True
    )
    grad_qkv = (
        qkv_share.astype(F32)
        .reshape(fc, piece, 3, width)
        .transpose(2, 1, 0, 3)
        .reshape(3, piece, D)
    )

    grad_input_part = jax.vjp(lambda z: norm_rows(z, gain_one), tokens.astype(F32))[1](
        grad_normed
    )[0]
    grad_tokens = grad_hidden + grad_input_part
    return (
        mixed,
        grad_tokens,
        grad_qkv,
        out_share,
        grad_gains,
        grad_table,
        grad_router,
        in_share,
        grad_w_out,
    )


def solution(mesh):
    return jax.shard_map(
        local,
        mesh=mesh,
        in_specs=(
            P(("rep", "fsdp"), None),
            P(("rep", "fsdp"), None),
            P("rep", None),
            P(),
            P(None, "fsdp", None),
            P("fsdp", None),
            P(None, "fsdp"),
            P("fsdp", None),
            P("fsdp", None),
            P(None, None, "fsdp"),
            P(None, "fsdp", None),
            P(("rep", "fsdp"), None),
        ),
        out_specs=(
            P(("rep", "fsdp"), None),
            P(("rep", "fsdp"), None),
            P(None, ("rep", "fsdp"), None),
            P(("rep", "fsdp"), None),
            P(None, "fsdp"),
            P("fsdp", None),
            P("fsdp", None),
            P(None, "rep", "fsdp"),
            P(None, ("rep", "fsdp"), None),
        ),
        check_vma=False,
    )
```
